256 devices in a mesh: grp: 8 (over y, core), ctx: 32 (over z, x).
Axes of the slice: x: 4, y: 4, z: 8, core: 2. Of those that a mesh axis runs over, the one named last changes fastest.
Arguments:
- queries: bfloat16 [512, 8192], P(('grp', 'ctx')), parts along dimension 0, may hold values from -12 to 12
- prefix_keys: bfloat16 [524288, 1024], P(('grp', 'ctx')), parts along dimension 0, may hold values from -8 to 8
- prefix_values: bfloat16 [524288, 1024], P(('grp', 'ctx')), parts along dimension 0, may hold values from -6 to 6
- suffix_keys: bfloat16 [512, 256, 1024], P(('grp', 'ctx')), parts along dimension 0, may hold values from -8 to 8
- suffix_values: bfloat16 [512, 256, 1024], P(('grp', 'ctx')), parts along dimension 0, may hold values from -6 to 6
- suffix_len: int32 [512], P(('grp', 'ctx')), parts along dimension 0, may hold values from 1 to 256, as said below
Outputs:
- attended: bfloat16 [512, 8192], P(('grp', 'ctx')), parts along dimension 0
The draws below stay inside these ranges and needn't reach their ends.
There are 8 independent parts, one for each index of `grp`. The reference program is written for one: setup_inputs(seed, part) draws one part's arguments, and reference() takes and returns one part's arrays. A program takes and returns all parts, laid end to end along the dimension named above; each array names one. Nothing has to cross between parts.
Inputs may be any that keep to these rules, and one draw needn't show every extreme that they name: `suffix_len`: some continuation has exactly 256 valid positions.
All inputs are finite; a program needn't handle non-finite values.
Results may differ from the reference program's by a relative error of at most 0.0055.
Values may be sent and summed in bfloat16 or wider, within the bound.
No kernel may reach another device: no remote copies, remote signals or barrier semaphores. Data moves between devices by JAX's collectives and lax.ppermute only.
A program may use at most 256 MiB of HBM per device.

```python
import jax
import jax.numpy as jnp
from jax import lax

H = 64
KVH = 8
HD = 128
CTX_DEV = 2048
SUF = 256
PREFIX = 65536
SAMPLES = 64
N_CTX = 32


def draw_queries(key, part):
    key = jax.random.fold_in(key, 11)
    first = jax.random.fold_in(key, 0)
    values = jnp.clip(jax.random.normal(first, (SAMPLES, H, HD), jnp.float32) * 3.0, -12.0, 12.0)
    return values.reshape(SAMPLES, H * HD).astype(jnp.bfloat16)


def draw_prefix_keys(key, part):
    key = jax.random.fold_in(key, 23)
    first = jax.random.fold_in(key, 0)
    values = jnp.clip(jax.random.normal(first, (PREFIX, KVH, HD), jnp.float32), -6.0, 6.0)
    return values.reshape(PREFIX, KVH * HD).astype(jnp.bfloat16)


def draw_suffix_len(key, part):
    key = jax.random.fold_in(key, 5)
    first, second = jax.random.split(key, 2)
    lengths = jax.random.randint(first, (SAMPLES,), 1, SUF + 1)
    lengths = jnp.maximum(lengths * lengths * lengths // (SUF * SUF), 1)
    chosen = jax.random.randint(second, (), 0, SAMPLES)
    lengths = jnp.where(jnp.arange(SAMPLES) == chosen, SUF, lengths)
    return lengths.astype(jnp.int32)


def level_of(stream_key, shape, pieces, low, largest):
    gain = 1.0
    for position, blocks in pieces:
        draws = jax.random.uniform(jax.random.fold_in(jax.random.fold_in(stream_key, 6), position), (blocks,), jnp.float32, low / len(pieces), largest / len(pieces))
        gain = gain * jnp.repeat(jnp.exp(draws), shape[position] // blocks).reshape((-1,) + (1,) * (len(shape) - 1 - position))
    return gain


def scatter_about(own_key, shape, spread, reach, shards=(), kind=jnp.bfloat16):
    values = spread * jax.random.normal(own_key, shape, jnp.float32)
    if shards:
        values = values * level_of(own_key, shape, shards, -0.22, 0.18)
    return jnp.clip(values, -reach, reach).astype(kind)


def setup_inputs(seed: int = 0, part: int = 0) -> dict:
    keys = jax.random.split(jax.random.key(seed), 7)
    own_keys = jax.random.split(jax.random.fold_in(keys[6], part), 7)
    return {
        "queries": draw_queries(jax.random.fold_in(jax.random.fold_in(keys[6], part), 71), part),
        "prefix_keys": draw_prefix_keys(jax.random.fold_in(jax.random.fold_in(keys[6], part), 71), part),
        "prefix_values": scatter_about(own_keys[2], (PREFIX, KVH * HD), 1.0, 6.0, ((0, 32),)),
        "suffix_keys": scatter_about(own_keys[3], (SAMPLES, SUF, KVH * HD), 1.4, 8.0, ((0, 32),)),
        "suffix_values": scatter_about(own_keys[4], (SAMPLES, SUF, KVH * HD), 1.0, 6.0, ((0, 32),)),
        "suffix_len": draw_suffix_len(jax.random.fold_in(jax.random.fold_in(keys[6], part), 71), part),
    }


NEG_FILL = -1e30


def prefix_block(queries, key_block, value_block):
    samples = queries.shape[0]
    kv_heads = key_block.shape[1] // HD
    group = queries.shape[1] // HD // kv_heads
    length = key_block.shape[0]
    query_heads = queries.astype(jnp.float32).reshape(samples, kv_heads, group, HD)
    key_heads = key_block.astype(jnp.float32).reshape(length, kv_heads, HD)
    value_heads = value_block.astype(jnp.float32).reshape(length, kv_heads, HD)
    scores = jnp.einsum("sgjd,cgd->sgjc", query_heads, key_heads) * (HD ** -0.5)
    block_max = jnp.max(scores, axis=3)
    weights = jnp.exp(scores - block_max[..., None]).astype(jnp.bfloat16)
    block_sum = jnp.sum(weights.astype(jnp.float32), axis=3)
    block_out = jnp.einsum("sgjc,cgd->sgjd", weights.astype(jnp.float32), value_heads)
    return block_max.reshape(samples, -1), block_sum.reshape(samples, -1), block_out.reshape(samples, -1)


def suffix_block(queries, suffix_keys, suffix_values, suffix_len):
    samples = suffix_keys.shape[0]
    length = suffix_keys.shape[1]
    kv_heads = suffix_keys.shape[2] // HD
    group = queries.shape[1] // HD // kv_heads
    query_heads = queries.astype(jnp.float32).reshape(samples, kv_heads, group, HD)
    key_heads = suffix_keys.astype(jnp.float32).reshape(samples, length, kv_heads, HD)
    value_heads = suffix_values.astype(jnp.float32).reshape(samples, length, kv_heads, HD)
    scores = jnp.einsum("sgjd,stgd->sgjt", query_heads, key_heads) * (HD ** -0.5)
    valid = jnp.arange(length, dtype=jnp.int32)[None, :] < suffix_len.astype(jnp.int32)[:, None]
    valid = valid[:, None, None, :]
    block_max = jnp.max(jnp.where(valid, scores, NEG_FILL), axis=3)
    weights = jnp.where(valid, jnp.exp(scores - block_max[..., None]), 0.0).astype(jnp.bfloat16)
    block_sum = jnp.sum(weights.astype(jnp.float32), axis=3)
    block_out = jnp.einsum("sgjt,stgd->sgjd", weights.astype(jnp.float32), value_heads)
    return block_max.reshape(samples, -1), block_sum.reshape(samples, -1), block_out.reshape(samples, -1)


def scale_heads(field, factor):
    dims = field.shape
    heads = factor.shape[-1]
    return (field.reshape(dims[:-1] + (heads, -1)) * factor[..., None]).reshape(dims)


def divide_heads(field, totals):
    dims = field.shape
    heads = totals.shape[-1]
    return (field.reshape(dims[:-1] + (heads, -1)) / totals[..., None]).reshape(dims)


def reference(queries, prefix_keys, prefix_values, suffix_keys, suffix_values, suffix_len):
    key_blocks = prefix_keys.reshape(N_CTX, CTX_DEV, -1)
    value_blocks = prefix_values.reshape(N_CTX, CTX_DEV, -1)

    def per_block(block_pair):
        return prefix_block(queries, block_pair[0], block_pair[1])

    pre_max, pre_sum, pre_out = lax.map(per_block, (key_blocks, value_blocks))
    suf_max, suf_sum, suf_out = suffix_block(queries, suffix_keys, suffix_values, suffix_len)
    row_top = jnp.maximum(jnp.max(pre_max, axis=0), suf_max)
    pre_factor = jnp.exp(pre_max - row_top[None])
    suf_factor = jnp.exp(suf_max - row_top)
    total_sum = jnp.sum(pre_sum * pre_factor, axis=0) + suf_sum * suf_factor
    total_out = jnp.sum(scale_heads(pre_out, pre_factor), axis=0) + scale_heads(suf_out, suf_factor)
    return divide_heads(total_out, total_sum).astype(jnp.bfloat16)
```

```python
import functools

import jax
import jax.numpy as jnp
from jax import lax
from jax.experimental import pallas as pl
from jax.experimental.pallas import tpu as pltpu
from jax.sharding import PartitionSpec as P

HD = 128
LOG2E = 1.4426950408889634
NEG_FILL = -1e30

NT = (((1,), (1,)), ((), ()))
NN = (((1,), (0,)), ((), ()))


def dot(a, b, dims):
    return lax.dot_general(a, b, dims, preferred_element_type=jnp.float32)


def to_lanes(column, head, rows):
    lane = lax.broadcasted_iota(jnp.int32, (rows, HD), 1)
    row = lax.broadcasted_iota(jnp.int32, (rows, HD), 0) % 16
    return jnp.where(lane == head * 16 + row, column, 0.0)


def prefix_kernel(factor, chunk, q_ref, k_ref, v_ref, out_ref, acc_max, acc_sum):
    head = pl.program_id(0)
    blocks = q_ref.shape[0]
    rows = blocks * 16
    keys = k_ref[...]
    values = jnp.concatenate([v_ref[...], jnp.ones_like(v_ref)], axis=1)
    for start in range(0, rows, chunk):
        part = slice(start // 16, (start + chunk) // 16)
        queries = q_ref[part].reshape(chunk, HD)
        scores = dot(queries, keys, NT)
        top = jnp.max(scores, axis=1, keepdims=True).astype(jnp.bfloat16).astype(jnp.float32)
        weights = jnp.exp2((scores - top) * factor).astype(jnp.bfloat16)
        both = dot(weights, values, NN)
        out_ref[part, head] = both[:, :HD].astype(jnp.bfloat16).reshape(chunk // 16, 16, HD)
        here = slice(start, start + chunk)
        new_max = to_lanes(top, head, chunk)
        new_sum = to_lanes(both[:, HD:], head, chunk)

        @pl.when(head == 0)
        def _():
            acc_max[here] = new_max
            acc_sum[here] = new_sum

        @pl.when(head > 0)
        def _():
            acc_max[here] += new_max
            acc_sum[here] += new_sum

    @pl.when(head == pl.num_programs(0) - 1)
    def _():
        tops = jnp.sum(acc_max[...].reshape(blocks, 16, HD), axis=1, keepdims=True)
        sums = jnp.sum(acc_sum[...].reshape(blocks, 16, HD), axis=1, keepdims=True)
        high = sums.astype(jnp.bfloat16).astype(jnp.float32)
        row = lax.broadcasted_iota(jnp.int32, (blocks, 16, HD), 1)
        stats = jnp.where(row == 0, tops, jnp.where(row == 1, high, jnp.where(row == 2, sums - high, 0.0)))
        out_ref[:, pl.num_programs(0)] = stats.astype(jnp.bfloat16)


def prefix_part(queries, keys, values, factor):
    blocks, heads = queries.shape[:2]
    length = keys.shape[0]
    rows = blocks * 16
    return pl.pallas_call(
        functools.partial(prefix_kernel, factor, min(rows, 256)),
        grid=(heads,),
        in_specs=[
            pl.BlockSpec((blocks, None, 16, HD), lambda g: (0, g, 0, 0)),
            pl.BlockSpec((length, HD), lambda g: (0, g)),
            pl.BlockSpec((length, HD), lambda g: (0, g)),
        ],
        out_specs=pl.BlockSpec((blocks, heads + 1, 16, HD), lambda g: (0, 0, 0, 0)),
        out_shape=jax.ShapeDtypeStruct((blocks, heads + 1, 16, HD), jnp.bfloat16),
        scratch_shapes=[pltpu.VMEM((rows, HD), jnp.float32)] * 2,
        compiler_params=pltpu.CompilerParams(vmem_limit_bytes=40 * 2**20),
        cost_estimate=pl.CostEstimate(
            flops=4 * rows * heads * length * HD,
            bytes_accessed=4 * length * heads * HD + 4 * rows * heads * HD,
            transcendentals=rows * heads * length,
        ),
        name="prefix_part",
    )(queries, keys, values)


def suffix_kernel(factor, len_ref, q_ref, k_ref, v_ref, out_ref, stat_ref):
    heads = q_ref.shape[0]
    length = k_ref.shape[1]
    odd = lax.broadcasted_iota(jnp.int32, (16, length), 0) % 2 == 1
    position = lax.broadcasted_iota(jnp.int32, (16, length), 1)
    valid = position < jnp.where(odd, len_ref[1], len_ref[0])
    maxima = jnp.zeros((16, HD), jnp.float32)
    sums = jnp.zeros((16, HD), jnp.float32)
    for head in range(heads):
        cols = slice(head * HD, (head + 1) * HD)
        queries = q_ref[head]
        scores = jnp.where(odd, dot(queries, k_ref[1, :, cols], NT), dot(queries, k_ref[0, :, cols], NT))
        top = jnp.max(jnp.where(valid, scores, NEG_FILL), axis=1, keepdims=True)
        weights = jnp.where(valid, jnp.exp2((scores - top) * factor), 0.0).astype(jnp.bfloat16)
        total = jnp.sum(weights.astype(jnp.float32), axis=1, keepdims=True)
        outs = jnp.where(odd[:, :HD], dot(weights, v_ref[1, :, cols], NN), dot(weights, v_ref[0, :, cols], NN))
        out_ref[head * 16:(head + 1) * 16] = outs
        maxima += to_lanes(top, head, 16)
        sums += to_lanes(total, head, 16)
    stat_ref[0:1] = jnp.sum(maxima, axis=0, keepdims=True)
    stat_ref[1:2] = jnp.sum(sums, axis=0, keepdims=True)
    stat_ref[2:] = jnp.zeros((6, HD), jnp.float32)


def suffix_part(lengths, queries, keys, values, factor):
    heads = queries.shape[0]
    vmem = pl.BlockSpec(memory_space=pltpu.VMEM)
    return pl.pallas_call(
        functools.partial(suffix_kernel, factor),
        in_specs=[pl.BlockSpec(memory_space=pltpu.SMEM), vmem, vmem, vmem],
        out_specs=[vmem, vmem],
        out_shape=[
            jax.ShapeDtypeStruct((heads * 16, HD), jnp.float32),
            jax.ShapeDtypeStruct((8, HD), jnp.float32),
        ],
        compiler_params=pltpu.CompilerParams(vmem_limit_bytes=16 * 2**20),
        name="suffix_part",
    )(lengths, queries, keys, values)


def combine_kernel(factor, got_ref, suf_ref, stat_ref, out_ref):
    blocks = got_ref.shape[0]
    heads = got_ref.shape[1] - 1
    stats = got_ref[:, heads].astype(jnp.float32)
    tops = stats[:, 0]
    sums = stats[:, 1] + stats[:, 2]
    suf_top = stat_ref[0:1]
    top = jnp.maximum(jnp.max(tops, axis=0, keepdims=True), suf_top)
    scale = jnp.exp2((tops - top) * factor)
    suf_scale = jnp.exp2((suf_top - top) * factor)
    total = jnp.sum(scale * sums, axis=0, keepdims=True) + suf_scale * stat_ref[1:2]
    shares = jnp.concatenate(
        [scale / total, suf_scale / total, jnp.zeros((HD - blocks - 1, HD), jnp.float32)], axis=0
    )
    shares = shares.T
    acc = suf_ref[...] * shares[:, blocks:blocks + 1]
    for src in range(blocks):
        block = got_ref[src, :heads].reshape(heads * 16, HD).astype(jnp.float32)
        acc += block * shares[:, src:src + 1]
    out_ref[...] = acc.astype(jnp.bfloat16)


def combine_part(got, suf_out, suf_stats, factor):
    vmem = pl.BlockSpec(memory_space=pltpu.VMEM)
    return pl.pallas_call(
        functools.partial(combine_kernel, factor),
        in_specs=[vmem, vmem, vmem],
        out_specs=vmem,
        out_shape=jax.ShapeDtypeStruct(suf_out.shape, jnp.bfloat16),
        compiler_params=pltpu.CompilerParams(vmem_limit_bytes=16 * 2**20),
        name="combine_part",
    )(got, suf_out, suf_stats)


def local(queries, prefix_keys, prefix_values, suffix_keys, suffix_values, suffix_len):
    owned, width = queries.shape
    heads = prefix_keys.shape[1] // HD
    factor = LOG2E * HD ** -0.5
    devices = lax.axis_size("ctx")
    mine = queries.reshape(owned, heads, 8, HD).transpose(1, 2, 0, 3).reshape(heads, 16, HD)
    copies = jnp.broadcast_to(mine[None], (devices,) + mine.shape)
    gathered = lax.all_to_all(copies, "ctx", 0, 0, tiled=True)
    suf_out, suf_stats = suffix_part(suffix_len, mine, suffix_keys, suffix_values, factor)
    partial = prefix_part(gathered, prefix_keys, prefix_values, factor)
    got = lax.all_to_all(partial, "ctx", 0, 0, tiled=True)
    out = combine_part(got, suf_out, suf_stats, factor)
    return out.reshape(heads * 8, owned, HD).transpose(1, 0, 2).reshape(owned, width)


def solution(mesh):
    placed = (
        P(("grp", "ctx"), None),
        P(("grp", "ctx"), None),
        P(("grp", "ctx"), None),
        P(("grp", "ctx"), None, None),
        P(("grp", "ctx"), None, None),
        P(("grp", "ctx")),
    )
    return jax.shard_map(
        local, mesh=mesh, in_specs=placed, out_specs=P(("grp", "ctx"), None), check_vma=False
    )
```

```python
import functools

import jax
import jax.numpy as jnp
from jax import lax
from jax.experimental import pallas as pl
from jax.experimental.pallas import tpu as pltpu
from jax.sharding import PartitionSpec as P

HD = 128
LOG2E = 1.4426950408889634
NEG_FILL = -1e30
ROWS = 16
Z, X = 8, 4

NT = (((1,), (1,)), ((), ()))
NN = (((1,), (0,)), ((), ()))
TN = (((0,), (0,)), ((), ()))
VMEM = pl.BlockSpec(memory_space=pltpu.VMEM)


def dot(a, b, dims):
    return lax.dot_general(a, b, dims, preferred_element_type=jnp.float32)


def rounded(x):
    return x.astype(jnp.bfloat16).astype(jnp.float32)


def by_device(field):
    row = lax.broadcasted_iota(jnp.int32, (8, HD), 0)
    group = lax.broadcasted_iota(jnp.int32, (8, HD), 1) // ROWS
    turn = (row - group) % 8
    out = field
    for k in range(1, 8):
        moved = pltpu.roll(pltpu.roll(field, k, 0), HD - ROWS * k, 1)
        out = jnp.where(turn == k, moved, out)
    return out


def stat_rows(tops, sums):
    devices = tops.shape[0]
    high = rounded(sums)
    row = lax.broadcasted_iota(jnp.int32, (devices, ROWS, HD), 1)
    low = jnp.where(row == 2, (sums - high)[:, None], 0.0)
    rows = jnp.where(row == 0, tops[:, None], jnp.where(row == 1, high[:, None], low))
    return rows.astype(jnp.bfloat16)


def read_stats(ref):
    stats = ref[:, ref.shape[1] - 1].astype(jnp.float32)
    return stats[:, 0], stats[:, 1] + stats[:, 2]


def columns(fields):
    used = sum(f.shape[0] for f in fields)
    return jnp.concatenate(list(fields) + [jnp.zeros((HD - used, HD), jnp.float32)], axis=0).T


def suffix_head(factor, head, lens, q_ref, k_ref, v_ref, out_ref, top_ref, sum_ref):
    length = k_ref.shape[1]
    lanes = pl.ds(pl.multiple_of(head * HD, HD), HD)
    odd = lax.broadcasted_iota(jnp.int32, (ROWS, length), 0) % 2 == 1
    position = lax.broadcasted_iota(jnp.int32, (ROWS, length), 1)
    valid = position < jnp.where(odd, lens[1], lens[0])
    queries = q_ref[head]
    scores = jnp.where(odd, dot(queries, k_ref[1, :, lanes], NT), dot(queries, k_ref[0, :, lanes], NT))
    top = jnp.max(jnp.where(valid, scores, NEG_FILL), axis=1, keepdims=True)
    weights = jnp.where(valid, jnp.exp2((scores - top) * factor), 0.0).astype(jnp.bfloat16)
    total = jnp.sum(weights.astype(jnp.float32), axis=1, keepdims=True)
    outs = jnp.where(odd[:, :HD], dot(weights, v_ref[1, :, lanes], NN), dot(weights, v_ref[0, :, lanes], NN))
    out_ref[pl.ds(pl.multiple_of(head * ROWS, ROWS), ROWS)] = outs
    lane = lax.broadcasted_iota(jnp.int32, (ROWS, HD), 1)
    row = lax.broadcasted_iota(jnp.int32, (ROWS, HD), 0)
    here = lane == head * ROWS + row
    top_ref[...] = jnp.where(here, top, top_ref[...])
    sum_ref[...] = jnp.where(here, total, sum_ref[...])


def prefix_kernel(factor, parts, with_suffix, *refs):
    refs = list(refs)
    take = lambda n: [refs.pop(0) for _ in range(n)]
    if with_suffix:
        suffix_in = take(4)
    else:
        take(1)
    q_refs = take(parts)
    k_ref, v_ref = take(2)
    out_refs = take(parts)
    if with_suffix:
        suf_ref, stat_ref = take(2)
    top_ref, sum_ref = take(2)
    devices, heads = q_refs[0].shape[:2]
    span = devices * ROWS
    length = k_ref.shape[0]

    def head_part(head, pieces, shift):
        step = length // pieces
        lanes = pl.ds(pl.multiple_of(head * HD, HD), HD)
        queries = jnp.concatenate([r[:, head].reshape(span, HD) for r in q_refs], axis=0)
        scores = [dot(k_ref[i * step:(i + 1) * step, lanes], queries, NT) for i in range(pieces)]
        top = rounded(jnp.max(scores[0][:shift], axis=0, keepdims=True))
        total = None
        for i in range(pieces):
            weights = jnp.exp2((scores[i] - top) * factor).astype(jnp.bfloat16)
            values = v_ref[i * step:(i + 1) * step, lanes]
            values = jnp.concatenate([values, jnp.ones((step, ROWS), jnp.bfloat16)], axis=1)
            more = dot(values, weights, TN)
            total = more if total is None else total + more
        outs = total[:HD].T.astype(jnp.bfloat16)
        for i in range(parts):
            out_refs[i][:, head] = outs[i * span:(i + 1) * span].reshape(devices, ROWS, HD)
        top_ref[pl.ds(head, 1)] = top
        sum_ref[pl.ds(head, 1)] = total[HD:HD + 1]

    if with_suffix:
        suf_top, suf_sum = take(2)
        suf_top[...] = jnp.zeros_like(suf_top)
        suf_sum[...] = jnp.zeros_like(suf_sum)
        lens = suffix_in[0][0], suffix_in[0][1]

    @pl.loop(0, heads // 4)
    def _(i):
        for j in range(4):
            head_part(i * 4 + j, 4, 256)
            if with_suffix:
                suffix_head(factor, i * 4 + j, lens, *suffix_in[1:], suf_ref, suf_top, suf_sum)

    @pl.when(jnp.logical_not(jnp.max(sum_ref[...]) < 2.0 ** 64))
    def _():
        @pl.loop(0, heads)
        def _(i):
            head_part(i, 1, length)

    for i in range(parts):
        part = slice(i * span, (i + 1) * span)
        out_refs[i][:, heads] = stat_rows(by_device(top_ref[:, part]), by_device(sum_ref[:, part]))
    if with_suffix:
        stat_ref[0:1] = jnp.sum(suf_top[...], axis=0, keepdims=True)
        stat_ref[1:2] = jnp.sum(suf_sum[...], axis=0, keepdims=True)
        stat_ref[2:] = jnp.zeros((6, HD), jnp.float32)


def prefix_part(queries, keys, values, factor, after=None, suffix=None):
    parts = len(queries)
    devices, heads = queries[0].shape[:2]
    length = keys.shape[0]
    rows = parts * devices * ROWS
    outs = [jax.ShapeDtypeStruct((devices, heads + 1, ROWS, HD), jnp.bfloat16)] * parts
    scratch = [pltpu.VMEM((heads, rows), jnp.float32)] * 2
    if suffix is None:
        first, first_specs = [after], [pl.BlockSpec(memory_space=pl.ANY)]
    else:
        first, first_specs = list(suffix), [pl.BlockSpec(memory_space=pltpu.SMEM), VMEM, VMEM, VMEM]
        outs += [jax.ShapeDtypeStruct((heads * ROWS, HD), jnp.float32), jax.ShapeDtypeStruct((8, HD), jnp.float32)]
        scratch += [pltpu.VMEM((ROWS, HD), jnp.float32)] * 2
    return pl.pallas_call(
        functools.partial(prefix_kernel, factor, parts, suffix is not None),
        in_specs=first_specs + [VMEM] * (parts + 2),
        out_specs=[VMEM] * len(outs),
        out_shape=outs,
        scratch_shapes=scratch,
        compiler_params=pltpu.CompilerParams(vmem_limit_bytes=32 * 2**20),
        cost_estimate=pl.CostEstimate(
            flops=8 * rows * heads * length * HD,
            bytes_accessed=4 * length * heads * HD + 4 * rows * heads * HD,
            transcendentals=rows * heads * length,
        ),
        name="prefix_part",
    )(*first, *queries, keys, values)


def merge_kernel(factor, *refs):
    part_refs, out_ref = refs[:-1], refs[-1]
    devices = out_ref.shape[0]
    heads = out_ref.shape[1] - 1
    stats = [read_stats(r) for r in part_refs]
    top = functools.reduce(jnp.maximum, [s[0] for s in stats])
    scales = [jnp.exp2((s[0] - top) * factor) for s in stats]
    out_ref[:, heads] = stat_rows(top, sum(f * s[1] for f, s in zip(scales, stats)))
    turned = columns(scales)
    for dev in range(devices):
        acc = None
        for i, r in enumerate(part_refs):
            block = r[dev, :heads].reshape(heads * ROWS, HD).astype(jnp.float32)
            term = block * turned[:, i * devices + dev:i * devices + dev + 1]
            acc = term if acc is None else acc + term
        out_ref[dev, :heads] = acc.astype(jnp.bfloat16).reshape(heads, ROWS, HD)


def merge_part(parts, factor):
    return pl.pallas_call(
        functools.partial(merge_kernel, factor),
        in_specs=[VMEM] * len(parts),
        out_specs=VMEM,
        out_shape=jax.ShapeDtypeStruct(parts[0].shape, jnp.bfloat16),
        compiler_params=pltpu.CompilerParams(vmem_limit_bytes=16 * 2**20),
        name="merge_part",
    )(*parts)


def touch_kernel(after_ref, k_ref, v_ref, out_ref):
    out_ref[...] = k_ref[:ROWS, :HD] + v_ref[:ROWS, :HD]


def touch_part(after, keys, values):
    return pl.pallas_call(
        touch_kernel,
        in_specs=[pl.BlockSpec(memory_space=pl.ANY), VMEM, VMEM],
        out_specs=VMEM,
        out_shape=jax.ShapeDtypeStruct((ROWS, HD), keys.dtype),
        compiler_params=pltpu.CompilerParams(vmem_limit_bytes=16 * 2**20),
        cost_estimate=pl.CostEstimate(flops=2**30, bytes_accessed=2**23, transcendentals=0),
        name="touch_part",
    )(after, keys, values)


def combine_kernel(factor, got_ref, suf_ref, stat_ref, out_ref):
    devices = got_ref.shape[0]
    heads = got_ref.shape[1] - 1
    tops, sums = read_stats(got_ref)
    suf_top = stat_ref[0:1]
    top = jnp.maximum(jnp.max(tops, axis=0, keepdims=True), suf_top)
    scale = jnp.exp2((tops - top) * factor)
    suf_scale = jnp.exp2((suf_top - top) * factor)
    total = jnp.sum(scale * sums, axis=0, keepdims=True) + suf_scale * stat_ref[1:2]
    shares = columns([scale / total, suf_scale / total])
    acc = suf_ref[...] * shares[:, devices:devices + 1]
    for src in range(devices):
        block = got_ref[src, :heads].reshape(heads * ROWS, HD).astype(jnp.float32)
        acc += block * shares[:, src:src + 1]
    out_ref[...] = acc.astype(jnp.bfloat16)


def combine_part(got, suf_out, suf_stats, factor):
    return pl.pallas_call(
        functools.partial(combine_kernel, factor),
        in_specs=[VMEM, VMEM, VMEM],
        out_specs=VMEM,
        out_shape=jax.ShapeDtypeStruct(suf_out.shape, jnp.bfloat16),
        compiler_params=pltpu.CompilerParams(vmem_limit_bytes=16 * 2**20),
        name="combine_part",
    )(got, suf_out, suf_stats)


def shift_x(array, by):
    pairs = [(z * X + x, z * X + (x + by) % X) for z in range(Z) for x in range(X)]
    return lax.ppermute(array, "ctx", pairs)


def swap_z(array):
    groups = [[z * X + x for z in range(Z)] for x in range(X)]
    return lax.all_to_all(array, "ctx", 0, 0, axis_index_groups=groups, tiled=True)


def local(queries, prefix_keys, prefix_values, suffix_keys, suffix_values, suffix_len):
    owned, width = queries.shape
    heads = prefix_keys.shape[1] // HD
    factor = LOG2E * HD ** -0.5
    mine = queries.reshape(owned, heads, 8, HD).transpose(1, 2, 0, 3).reshape(heads, ROWS, HD)
    column = swap_z(jnp.broadcast_to(mine[None], (Z,) + mine.shape))
    before, after = shift_x(column, 1), shift_x(column, -1)
    ready = touch_part(column, prefix_keys, prefix_values)
    column, before, after = lax.optimization_barrier((column, before, after))
    across = shift_x(column, 2)
    for_before, for_after = prefix_part([before, after], prefix_keys, prefix_values, factor, after=ready)
    from_after, from_before = shift_x(for_before, -1), shift_x(for_after, 1)
    suffix = suffix_len, mine, suffix_keys, suffix_values
    for_own, for_across, suf_out, suf_stats = prefix_part(
        [column, across], prefix_keys, prefix_values, factor, suffix=suffix
    )
    from_across = shift_x(for_across, 2)
    merged = merge_part([for_own, from_after, from_before, from_across], factor)
    got = swap_z(merged)
    out = combine_part(got, suf_out, suf_stats, factor)
    return out.reshape(heads * 8, owned, HD).transpose(1, 0, 2).reshape(owned, width)


def solution(mesh):
    placed = (
        P(("grp", "ctx"), None),
        P(("grp", "ctx"), None),
        P(("grp", "ctx"), None),
        P(("grp", "ctx"), None, None),
        P(("grp", "ctx"), None, None),
        P(("grp", "ctx")),
    )
    return jax.shard_map(
        local, mesh=mesh, in_specs=placed, out_specs=P(("grp", "ctx"), None), check_vma=False
    )
```

```python
import functools

import jax
import jax.numpy as jnp
from jax import lax
from jax.experimental import pallas as pl
from jax.experimental.pallas import tpu as pltpu
from jax.sharding import PartitionSpec as P

HD = 128
LOG2E = 1.4426950408889634
NEG_FILL = -1e30
ROWS = 16
Z, X = 8, 4

NT = (((1,), (1,)), ((), ()))
NN = (((1,), (0,)), ((), ()))
TN = (((0,), (0,)), ((), ()))
VMEM = pl.BlockSpec(memory_space=pltpu.VMEM)


def dot(a, b, dims):
    return lax.dot_general(a, b, dims, preferred_element_type=jnp.float32)


def rounded(x):
    return x.astype(jnp.bfloat16).astype(jnp.float32)


def by_device(field):
    row = lax.broadcasted_iota(jnp.int32, (8, HD), 0)
    group = lax.broadcasted_iota(jnp.int32, (8, HD), 1) // ROWS
    turn = (row - group) % 8
    out = field
    for k in range(1, 8):
        moved = pltpu.roll(pltpu.roll(field, k, 0), HD - ROWS * k, 1)
        out = jnp.where(turn == k, moved, out)
    return out


def stat_rows(tops, sums):
    devices = tops.shape[0]
    high = rounded(sums)
    row = lax.broadcasted_iota(jnp.int32, (devices, ROWS, HD), 1)
    low = jnp.where(row == 2, (sums - high)[:, None], 0.0)
    rows = jnp.where(row == 0, tops[:, None], jnp.where(row == 1, high[:, None], low))
    return rows.astype(jnp.bfloat16)


def read_stats(ref):
    stats = ref[:, ref.shape[1] - 1].astype(jnp.float32)
    return stats[:, 0], stats[:, 1] + stats[:, 2]


def columns(fields):
    used = sum(f.shape[0] for f in fields)
    return jnp.concatenate(list(fields) + [jnp.zeros((HD - used, HD), jnp.float32)], axis=0).T


def prefix_kernel(factor, parts, after_ref, *refs):
    q_refs = refs[:parts]
    k_ref, v_ref = refs[parts:parts + 2]
    out_refs = refs[parts + 2:2 * parts + 2]
    top_ref, sum_ref = refs[2 * parts + 2:]
    devices, heads = q_refs[0].shape[:2]
    span = devices * ROWS
    length = k_ref.shape[0]

    def head_part(head, pieces, shift):
        step = length // pieces
        lanes = pl.ds(pl.multiple_of(head * HD, HD), HD)
        queries = jnp.concatenate([r[:, head].reshape(span, HD) for r in q_refs], axis=0)
        scores = [dot(k_ref[i * step:(i + 1) * step, lanes], queries, NT) for i in range(pieces)]
        top = rounded(jnp.max(scores[0][:shift], axis=0, keepdims=True))
        total = None
        for i in range(pieces):
            weights = jnp.exp2((scores[i] - top) * factor).astype(jnp.bfloat16)
            values = v_ref[i * step:(i + 1) * step, lanes]
            values = jnp.concatenate([values, jnp.ones((step, ROWS), jnp.bfloat16)], axis=1)
            more = dot(values, weights, TN)
            total = more if total is None else total + more
        outs = total[:HD].T.astype(jnp.bfloat16)
        for i in range(parts):
            out_refs[i][:, head] = outs[i * span:(i + 1) * span].reshape(devices, ROWS, HD)
        top_ref[pl.ds(head, 1)] = top
        sum_ref[pl.ds(head, 1)] = total[HD:HD + 1]

    @pl.loop(0, heads // 4)
    def _(i):
        for j in range(4):
            head_part(i * 4 + j, 4, 256)

    @pl.when(jnp.logical_not(jnp.max(sum_ref[...]) < 2.0 ** 64))
    def _():
        @pl.loop(0, heads)
        def _(i):
            head_part(i, 1, length)

    for i in range(parts):
        part = slice(i * span, (i + 1) * span)
        out_refs[i][:, heads] = stat_rows(by_device(top_ref[:, part]), by_device(sum_ref[:, part]))


def prefix_part(after, queries, keys, values, factor):
    parts = len(queries)
    devices, heads = queries[0].shape[:2]
    length = keys.shape[0]
    rows = parts * devices * ROWS
    return pl.pallas_call(
        functools.partial(prefix_kernel, factor, parts),
        in_specs=[pl.BlockSpec(memory_space=pl.ANY)] + [VMEM] * (parts + 2),
        out_specs=[VMEM] * parts,
        out_shape=[jax.ShapeDtypeStruct((devices, heads + 1, ROWS, HD), jnp.bfloat16)] * parts,
        scratch_shapes=[pltpu.VMEM((heads, rows), jnp.float32)] * 2,
        compiler_params=pltpu.CompilerParams(vmem_limit_bytes=32 * 2**20),
        cost_estimate=pl.CostEstimate(
            flops=8 * rows * heads * length * HD,
            bytes_accessed=4 * length * heads * HD + 4 * rows * heads * HD,
            transcendentals=rows * heads * length,
        ),
        name="prefix_part",
    )(after, *queries, keys, values)


def spread_kernel(q_ref, out_ref):
    for i in range(out_ref.shape[0]):
        out_ref[i] = q_ref[...]


def spread_part(queries, copies):
    return pl.pallas_call(
        spread_kernel,
        in_specs=[VMEM],
        out_specs=VMEM,
        out_shape=jax.ShapeDtypeStruct((copies,) + queries.shape, queries.dtype),
        compiler_params=pltpu.CompilerParams(vmem_limit_bytes=8 * 2**20),
        cost_estimate=pl.CostEstimate(flops=20 * 2**30, bytes_accessed=2**25, transcendentals=0),
        name="spread_part",
    )(queries)


def suffix_kernel(factor, len_ref, after_ref, q_ref, sk_ref, sv_ref, k_ref, v_ref, out_ref, stat_ref):
    heads = q_ref.shape[0]
    length = sk_ref.shape[1]
    odd = lax.broadcasted_iota(jnp.int32, (ROWS, length), 0) % 2 == 1
    position = lax.broadcasted_iota(jnp.int32, (ROWS, length), 1)
    valid = position < jnp.where(odd, len_ref[1], len_ref[0])
    lane = lax.broadcasted_iota(jnp.int32, (ROWS, HD), 1)
    row = lax.broadcasted_iota(jnp.int32, (ROWS, HD), 0)
    maxima = jnp.zeros((ROWS, HD), jnp.float32)
    sums = jnp.zeros((ROWS, HD), jnp.float32)
    for head in range(heads):
        cols = slice(head * HD, (head + 1) * HD)
        queries = q_ref[head]
        scores = jnp.where(odd, dot(queries, sk_ref[1, :, cols], NT), dot(queries, sk_ref[0, :, cols], NT))
        top = jnp.max(jnp.where(valid, scores, NEG_FILL), axis=1, keepdims=True)
        weights = jnp.where(valid, jnp.exp2((scores - top) * factor), 0.0).astype(jnp.bfloat16)
        total = jnp.sum(weights.astype(jnp.float32), axis=1, keepdims=True)
        outs = jnp.where(odd[:, :HD], dot(weights, sv_ref[1, :, cols], NN), dot(weights, sv_ref[0, :, cols], NN))
        out_ref[head * ROWS:(head + 1) * ROWS] = outs
        here = lane == head * ROWS + row
        maxima += jnp.where(here, top, 0.0)
        sums += jnp.where(here, total, 0.0)
    stat_ref[0:1] = jnp.sum(maxima, axis=0, keepdims=True)
    stat_ref[1:2] = jnp.sum(sums, axis=0, keepdims=True)
    stat_ref[2:] = jnp.zeros((6, HD), jnp.float32)


def suffix_part(lengths, after, queries, suffix_keys, suffix_values, keys, values, factor):
    heads = queries.shape[0]
    return pl.pallas_call(
        functools.partial(suffix_kernel, factor),
        in_specs=[pl.BlockSpec(memory_space=pltpu.SMEM), pl.BlockSpec(memory_space=pl.ANY)] + [VMEM] * 5,
        out_specs=[VMEM] * 2,
        out_shape=[
            jax.ShapeDtypeStruct((heads * ROWS, HD), jnp.float32),
            jax.ShapeDtypeStruct((8, HD), jnp.float32),
        ],
        compiler_params=pltpu.CompilerParams(vmem_limit_bytes=16 * 2**20),
        cost_estimate=pl.CostEstimate(flops=2**30, bytes_accessed=2**23, transcendentals=2**16),
        name="suffix_part",
    )(lengths, after, queries, suffix_keys, suffix_values, keys, values)


def merge_kernel(factor, *refs):
    part_refs, out_ref = refs[:-1], refs[-1]
    devices = out_ref.shape[0]
    heads = out_ref.shape[1] - 1
    stats = [read_stats(r) for r in part_refs]
    top = functools.reduce(jnp.maximum, [s[0] for s in stats])
    scales = [jnp.exp2((s[0] - top) * factor) for s in stats]
    out_ref[:, heads] = stat_rows(top, sum(f * s[1] for f, s in zip(scales, stats)))
    turned = columns(scales)
    for dev in range(devices):
        acc = None
        for i, r in enumerate(part_refs):
            block = r[dev, :heads].reshape(heads * ROWS, HD).astype(jnp.float32)
            term = block * turned[:, i * devices + dev:i * devices + dev + 1]
            acc = term if acc is None else acc + term
        out_ref[dev, :heads] = acc.astype(jnp.bfloat16).reshape(heads, ROWS, HD)


def merge_part(parts, factor):
    return pl.pallas_call(
        functools.partial(merge_kernel, factor),
        in_specs=[VMEM] * len(parts),
        out_specs=VMEM,
        out_shape=jax.ShapeDtypeStruct(parts[0].shape, jnp.bfloat16),
        compiler_params=pltpu.CompilerParams(vmem_limit_bytes=16 * 2**20),
        name="merge_part",
    )(*parts)


def combine_kernel(factor, got_ref, suf_ref, stat_ref, out_ref):
    devices = got_ref.shape[0]
    heads = got_ref.shape[1] - 1
    tops, sums = read_stats(got_ref)
    suf_top = stat_ref[0:1]
    top = jnp.maximum(jnp.max(tops, axis=0, keepdims=True), suf_top)
    scale = jnp.exp2((tops - top) * factor)
    suf_scale = jnp.exp2((suf_top - top) * factor)
    total = jnp.sum(scale * sums, axis=0, keepdims=True) + suf_scale * stat_ref[1:2]
    shares = columns([scale / total, suf_scale / total])
    acc = suf_ref[...] * shares[:, devices:devices + 1]
    for src in range(devices):
        block = got_ref[src, :heads].reshape(heads * ROWS, HD).astype(jnp.float32)
        acc += block * shares[:, src:src + 1]
    out_ref[...] = acc.astype(jnp.bfloat16)


def combine_part(got, suf_out, suf_stats, factor):
    return pl.pallas_call(
        functools.partial(combine_kernel, factor),
        in_specs=[VMEM, VMEM, VMEM],
        out_specs=VMEM,
        out_shape=jax.ShapeDtypeStruct(suf_out.shape, jnp.bfloat16),
        compiler_params=pltpu.CompilerParams(vmem_limit_bytes=16 * 2**20),
        name="combine_part",
    )(got, suf_out, suf_stats)


def shift_x(array, by):
    pairs = [(z * X + x, z * X + (x + by) % X) for z in range(Z) for x in range(X)]
    return lax.ppermute(array, "ctx", pairs)


def swap_z(array):
    groups = [[z * X + x for z in range(Z)] for x in range(X)]
    return lax.all_to_all(array, "ctx", 0, 0, axis_index_groups=groups, tiled=True)


def local(queries, prefix_keys, prefix_values, suffix_keys, suffix_values, suffix_len):
    owned, width = queries.shape
    heads = prefix_keys.shape[1] // HD
    factor = LOG2E * HD ** -0.5
    mine = queries.reshape(owned, heads, 8, HD).transpose(1, 2, 0, 3).reshape(heads, ROWS, HD)
    column = swap_z(spread_part(mine, Z))
    before, after = shift_x(column, 1), shift_x(column, -1)
    suf_out, suf_stats = suffix_part(
        suffix_len, column, mine, suffix_keys, suffix_values, prefix_keys, prefix_values, factor
    )
    column, before, after = lax.optimization_barrier((column, before, after))
    across = shift_x(column, 2)
    for_before, for_after = prefix_part(suf_stats, [before, after], prefix_keys, prefix_values, factor)
    from_after, from_before = shift_x(for_before, -1), shift_x(for_after, 1)
    for_own, for_across = prefix_part(suf_stats, [column, across], prefix_keys, prefix_values, factor)
    from_across = shift_x(for_across, 2)
    merged = merge_part([for_own, from_after, from_before, from_across], factor)
    got = swap_z(merged)
    out = combine_part(got, suf_out, suf_stats, factor)
    return out.reshape(heads * 8, owned, HD).transpose(1, 0, 2).reshape(owned, width)


def solution(mesh):
    placed = (
        P(("grp", "ctx"), None),
        P(("grp", "ctx"), None),
        P(("grp", "ctx"), None),
        P(("grp", "ctx"), None, None),
        P(("grp", "ctx"), None, None),
        P(("grp", "ctx")),
    )
    return jax.shard_map(
        local, mesh=mesh, in_specs=placed, out_specs=P(("grp", "ctx"), None), check_vma=False
    )
```

```python
import functools

import jax
import jax.numpy as jnp
from jax import lax
from jax.experimental import pallas as pl
from jax.experimental.pallas import tpu as pltpu
from jax.sharding import PartitionSpec as P

HD = 128
LOG2E = 1.4426950408889634
NEG_FILL = -1e30
ROWS = 16
Z, X = 8, 4

NT = (((1,), (1,)), ((), ()))
NN = (((1,), (0,)), ((), ()))
TN = (((0,), (0,)), ((), ()))
VMEM = pl.BlockSpec(memory_space=pltpu.VMEM)


def dot(a, b, dims):
    return lax.dot_general(a, b, dims, preferred_element_type=jnp.float32)


def rounded(x):
    return x.astype(jnp.bfloat16).astype(jnp.float32)


def by_device(field):
    row = lax.broadcasted_iota(jnp.int32, (8, HD), 0)
    group = lax.broadcasted_iota(jnp.int32, (8, HD), 1) // ROWS
    turn = (row - group) % 8
    out = field
    for k in range(1, 8):
        moved = pltpu.roll(pltpu.roll(field, k, 0), HD - ROWS * k, 1)
        out = jnp.where(turn == k, moved, out)
    return out


def stat_rows(tops, sums):
    devices = tops.shape[0]
    high = rounded(sums)
    row = lax.broadcasted_iota(jnp.int32, (devices, ROWS, HD), 1)
    low = jnp.where(row == 2, (sums - high)[:, None], 0.0)
    rows = jnp.where(row == 0, tops[:, None], jnp.where(row == 1, high[:, None], low))
    return rows.astype(jnp.bfloat16)


def read_stats(ref):
    stats = ref[:, ref.shape[1] - 1].astype(jnp.float32)
    return stats[:, 0], stats[:, 1] + stats[:, 2]


def write_packed_stats(ref, tops, sums):
    last = ref.shape[0] - 2
    high = rounded(sums)
    ref[last] = jnp.concatenate([tops, high], axis=0).astype(jnp.bfloat16)
    ref[last + 1] = jnp.concatenate([sums - high, jnp.zeros_like(sums)], axis=0).astype(jnp.bfloat16)


def read_packed_stats(ref):
    last = ref.shape[0] - 2
    first, second = ref[last].astype(jnp.float32), ref[last + 1].astype(jnp.float32)
    return first[:8], first[8:] + second[:8]


def columns(fields):
    used = sum(f.shape[0] for f in fields)
    return jnp.concatenate(list(fields) + [jnp.zeros((HD - used, HD), jnp.float32)], axis=0).T


def prefix_kernel(factor, parts, after_ref, *refs):
    q_refs = refs[:parts]
    k_ref, v_ref = refs[parts:parts + 2]
    out_refs = refs[parts + 2:2 * parts + 2]
    top_ref, sum_ref = refs[2 * parts + 2:]
    devices, heads = q_refs[0].shape[:2]
    span = devices * ROWS
    length = k_ref.shape[0]

    def pair_part(pair, pieces, shift):
        step = length // pieces
        lanes = slice(pair * 2 * HD, (pair + 1) * 2 * HD)
        both = [q_refs[0][:, pair * 2 + j].reshape(span, HD) for j in range(2)]
        none = jnp.zeros_like(both[0])
        queries = jnp.concatenate(
            [jnp.concatenate([both[0], none], axis=1), jnp.concatenate([none, both[1]], axis=1)], axis=0
        )
        scores = [dot(k_ref[i * step:(i + 1) * step, lanes], queries, NT) for i in range(pieces)]
        top = rounded(jnp.max(scores[0][:shift], axis=0, keepdims=True))
        total = None
        for i in range(pieces):
            weights = jnp.exp2((scores[i] - top) * factor).astype(jnp.bfloat16)
            values = v_ref[i * step:(i + 1) * step, lanes]
            values = jnp.concatenate([values, jnp.ones((step, ROWS), jnp.bfloat16)], axis=1)
            more = dot(values, weights, TN)
            total = more if total is None else total + more
        for j in range(2):
            head, cols = pair * 2 + j, slice(j * span, (j + 1) * span)
            outs = total[j * HD:(j + 1) * HD, cols].T.astype(jnp.bfloat16)
            for dev in range(devices):
                out_refs[0][dev * heads + head] = outs[dev * ROWS:(dev + 1) * ROWS]
            top_ref[pl.ds(head, 1)] = top[:, cols]
            sum_ref[pl.ds(head, 1)] = total[2 * HD:2 * HD + 1, cols]

    def head_part(head, pieces, shift):
        step = length // pieces
        lanes = slice(head * HD, (head + 1) * HD) if isinstance(head, int) else pl.ds(pl.multiple_of(head * HD, HD), HD)
        queries = jnp.concatenate([r[:, head].reshape(span, HD) for r in q_refs], axis=0)
        scores = [dot(k_ref[i * step:(i + 1) * step, lanes], queries, NT) for i in range(pieces)]
        top = rounded(jnp.max(scores[0][:shift], axis=0, keepdims=True))
        total = None
        for i in range(pieces):
            weights = jnp.exp2((scores[i] - top) * factor).astype(jnp.bfloat16)
            values = v_ref[i * step:(i + 1) * step, lanes]
            values = jnp.concatenate([values, jnp.ones((step, ROWS), jnp.bfloat16)], axis=1)
            more = dot(values, weights, TN)
            total = more if total is None else total + more
        outs = total[:HD].T.astype(jnp.bfloat16)
        for i in range(parts):
            for dev in range(devices):
                first = i * span + dev * ROWS
                out_refs[i][dev * heads + head] = outs[first:first + ROWS]
        top_ref[pl.ds(head, 1)] = top
        sum_ref[pl.ds(head, 1)] = total[HD:HD + 1]

    if parts == 1:
        for pair in range(heads // 2):
            pair_part(pair, 8, 128)
    else:
        for head in range(heads):
            head_part(head, 4, 64)

    @pl.when(jnp.logical_not(jnp.max(sum_ref[...]) < 2.0 ** 64))
    def _():
        @pl.loop(0, heads)
        def _(i):
            head_part(i, 1, length)

    for i in range(parts):
        part = slice(i * span, (i + 1) * span)
        write_packed_stats(out_refs[i], by_device(top_ref[:, part]), by_device(sum_ref[:, part]))


def prefix_part(after, queries, keys, values, factor, cost=1.0):
    parts = len(queries)
    devices, heads = queries[0].shape[:2]
    length = keys.shape[0]
    rows = parts * devices * ROWS
    return pl.pallas_call(
        functools.partial(prefix_kernel, factor, parts),
        in_specs=[pl.BlockSpec(memory_space=pl.ANY)] + [VMEM] * (parts + 2),
        out_specs=[VMEM] * parts,
        out_shape=[jax.ShapeDtypeStruct((devices * heads + 2, ROWS, HD), jnp.bfloat16)] * parts,
        scratch_shapes=[pltpu.VMEM((heads, rows), jnp.float32)] * 2,
        compiler_params=pltpu.CompilerParams(vmem_limit_bytes=32 * 2**20),
        cost_estimate=pl.CostEstimate(
            flops=int(cost * 8 * rows * heads * length * HD),
            bytes_accessed=int(cost * 4 * (length + rows) * heads * HD),
            transcendentals=int(cost * rows * heads * length),
        ),
        name="prefix_part",
    )(after, *queries, keys, values)


def spread_kernel(q_ref, out_ref):
    for i in range(out_ref.shape[0]):
        out_ref[i] = q_ref[...]


def spread_part(queries, copies):
    return pl.pallas_call(
        spread_kernel,
        in_specs=[VMEM],
        out_specs=VMEM,
        out_shape=jax.ShapeDtypeStruct((copies,) + queries.shape, queries.dtype),
        compiler_params=pltpu.CompilerParams(vmem_limit_bytes=8 * 2**20),
        cost_estimate=pl.CostEstimate(flops=20 * 2**30, bytes_accessed=2**25, transcendentals=0),
        name="spread_part",
    )(queries)


def suffix_kernel(factor, len_ref, after_ref, q_ref, sk_ref, sv_ref, k_ref, v_ref, out_ref, stat_ref):
    heads = q_ref.shape[0]
    length = sk_ref.shape[1]
    odd = lax.broadcasted_iota(jnp.int32, (ROWS, length), 0) % 2 == 1
    position = lax.broadcasted_iota(jnp.int32, (ROWS, length), 1)
    valid = position < jnp.where(odd, len_ref[1], len_ref[0])
    lane = lax.broadcasted_iota(jnp.int32, (ROWS, HD), 1)
    row = lax.broadcasted_iota(jnp.int32, (ROWS, HD), 0)
    maxima = jnp.zeros((ROWS, HD), jnp.float32)
    sums = jnp.zeros((ROWS, HD), jnp.float32)
    for head in range(heads):
        cols = slice(head * HD, (head + 1) * HD)
        queries = q_ref[head]
        scores = jnp.where(odd, dot(queries, sk_ref[1, :, cols], NT), dot(queries, sk_ref[0, :, cols], NT))
        top = jnp.max(jnp.where(valid, scores, NEG_FILL), axis=1, keepdims=True)
        weights = jnp.where(valid, jnp.exp2((scores - top) * factor), 0.0).astype(jnp.bfloat16)
        total = jnp.sum(weights.astype(jnp.float32), axis=1, keepdims=True)
        outs = jnp.where(odd[:, :HD], dot(weights, sv_ref[1, :, cols], NN), dot(weights, sv_ref[0, :, cols], NN))
        out_ref[head * ROWS:(head + 1) * ROWS] = outs
        here = lane == head * ROWS + row
        maxima += jnp.where(here, top, 0.0)
        sums += jnp.where(here, total, 0.0)
    stat_ref[0:1] = jnp.sum(maxima, axis=0, keepdims=True)
    stat_ref[1:2] = jnp.sum(sums, axis=0, keepdims=True)
    stat_ref[2:] = jnp.zeros((6, HD), jnp.float32)


def suffix_part(lengths, after, queries, suffix_keys, suffix_values, keys, values, factor):
    heads = queries.shape[0]
    return pl.pallas_call(
        functools.partial(suffix_kernel, factor),
        in_specs=[pl.BlockSpec(memory_space=pltpu.SMEM), pl.BlockSpec(memory_space=pl.ANY)] + [VMEM] * 5,
        out_specs=[VMEM] * 2,
        out_shape=[
            jax.ShapeDtypeStruct((heads * ROWS, HD), jnp.float32),
            jax.ShapeDtypeStruct((8, HD), jnp.float32),
        ],
        compiler_params=pltpu.CompilerParams(vmem_limit_bytes=16 * 2**20),
        cost_estimate=pl.CostEstimate(flops=2**30, bytes_accessed=2**23, transcendentals=2**16),
        name="suffix_part",
    )(lengths, after, queries, suffix_keys, suffix_values, keys, values)


def merge_kernel(factor, *refs):
    part_refs, out_ref = refs[:-1], refs[-1]
    devices = out_ref.shape[0]
    heads = out_ref.shape[1] - 1
    stats = [read_packed_stats(r) for r in part_refs]
    top = functools.reduce(jnp.maximum, [s[0] for s in stats])
    scales = [jnp.exp2((s[0] - top) * factor) for s in stats]
    out_ref[:, heads] = stat_rows(top, sum(f * s[1] for f, s in zip(scales, stats)))
    turned = columns(scales)
    for dev in range(devices):
        acc = None
        for i, r in enumerate(part_refs):
            block = r[dev * heads:(dev + 1) * heads].reshape(heads * ROWS, HD).astype(jnp.float32)
            term = block * turned[:, i * devices + dev:i * devices + dev + 1]
            acc = term if acc is None else acc + term
        out_ref[dev, :heads] = acc.astype(jnp.bfloat16).reshape(heads, ROWS, HD)


def merge_part(parts, factor):
    return pl.pallas_call(
        functools.partial(merge_kernel, factor),
        in_specs=[VMEM] * len(parts),
        out_specs=VMEM,
        out_shape=jax.ShapeDtypeStruct((Z, parts[0].shape[0] // Z + 1, ROWS, HD), jnp.bfloat16),
        compiler_params=pltpu.CompilerParams(vmem_limit_bytes=16 * 2**20),
        name="merge_part",
    )(*parts)


def combine_kernel(factor, got_ref, suf_ref, stat_ref, out_ref):
    devices = got_ref.shape[0]
    heads = got_ref.shape[1] - 1
    tops, sums = read_stats(got_ref)
    suf_top = stat_ref[0:1]
    top = jnp.maximum(jnp.max(tops, axis=0, keepdims=True), suf_top)
    scale = jnp.exp2((tops - top) * factor)
    suf_scale = jnp.exp2((suf_top - top) * factor)
    total = jnp.sum(scale * sums, axis=0, keepdims=True) + suf_scale * stat_ref[1:2]
    shares = columns([scale / total, suf_scale / total])
    acc = suf_ref[...] * shares[:, devices:devices + 1]
    for src in range(devices):
        block = got_ref[src, :heads].reshape(heads * ROWS, HD).astype(jnp.float32)
        acc += block * shares[:, src:src + 1]
    out_ref[...] = acc.astype(jnp.bfloat16)


def combine_part(got, suf_out, suf_stats, factor):
    return pl.pallas_call(
        functools.partial(combine_kernel, factor),
        in_specs=[VMEM, VMEM, VMEM],
        out_specs=VMEM,
        out_shape=jax.ShapeDtypeStruct(suf_out.shape, jnp.bfloat16),
        compiler_params=pltpu.CompilerParams(vmem_limit_bytes=16 * 2**20),
        name="combine_part",
    )(got, suf_out, suf_stats)


def shift_x(array, by):
    pairs = [(z * X + x, z * X + (x + by) % X) for z in range(Z) for x in range(X)]
    return lax.ppermute(array, "ctx", pairs)


def swap_z(array):
    groups = [[z * X + x for z in range(Z)] for x in range(X)]
    return lax.all_to_all(array, "ctx", 0, 0, axis_index_groups=groups, tiled=True)


def local(queries, prefix_keys, prefix_values, suffix_keys, suffix_values, suffix_len):
    owned, width = queries.shape
    heads = prefix_keys.shape[1] // HD
    factor = LOG2E * HD ** -0.5
    mine = queries.reshape(owned, heads, 8, HD).transpose(1, 2, 0, 3).reshape(heads, ROWS, HD)
    column = swap_z(spread_part(mine, Z))
    before, after = shift_x(column, 1), shift_x(column, -1)
    suf_out, suf_stats = suffix_part(
        suffix_len, column, mine, suffix_keys, suffix_values, prefix_keys, prefix_values, factor
    )
    across = shift_x(before, 1)
    for_before, for_after = prefix_part(suf_stats, [before, after], prefix_keys, prefix_values, factor)
    from_after, from_before = shift_x(for_before, -1), shift_x(for_after, 1)
    [for_across] = prefix_part(for_before, [across], prefix_keys, prefix_values, factor)
    from_across = shift_x(for_across, 2)
    [for_own] = prefix_part(for_across, [column], prefix_keys, prefix_values, factor, cost=0.01)
    merged = merge_part([for_own, from_after, from_before, from_across], factor)
    got = swap_z(merged)
    out = combine_part(got, suf_out, suf_stats, factor)
    return out.reshape(heads * 8, owned, HD).transpose(1, 0, 2).reshape(owned, width)


def solution(mesh):
    placed = (
        P(("grp", "ctx"), None),
        P(("grp", "ctx"), None),
        P(("grp", "ctx"), None),
        P(("grp", "ctx"), None, None),
        P(("grp", "ctx"), None, None),
        P(("grp", "ctx")),
    )
    return jax.shard_map(
        local, mesh=mesh, in_specs=placed, out_specs=P(("grp", "ctx"), None), check_vma=False
    )
```

```python
import functools

import jax
import jax.numpy as jnp
from jax import lax
from jax.experimental import pallas as pl
from jax.experimental.pallas import tpu as pltpu
from jax.sharding import PartitionSpec as P

HD = 128
LOG2E = 1.4426950408889634
NEG_FILL = -1e30
ROWS = 16
Z, X = 8, 4

NT = (((1,), (1,)), ((), ()))
NN = (((1,), (0,)), ((), ()))
TN = (((0,), (0,)), ((), ()))
VMEM = pl.BlockSpec(memory_space=pltpu.VMEM)


def dot(a, b, dims):
    return lax.dot_general(a, b, dims, preferred_element_type=jnp.float32)


def rounded(x):
    return x.astype(jnp.bfloat16).astype(jnp.float32)


def by_device(field):
    row = lax.broadcasted_iota(jnp.int32, (8, HD), 0)
    group = lax.broadcasted_iota(jnp.int32, (8, HD), 1) // ROWS
    turn = (row - group) % 8
    out = field
    for k in range(1, 8):
        moved = pltpu.roll(pltpu.roll(field, k, 0), HD - ROWS * k, 1)
        out = jnp.where(turn == k, moved, out)
    return out


def stat_rows(tops, sums):
    devices = tops.shape[0]
    high = rounded(sums)
    row = lax.broadcasted_iota(jnp.int32, (devices, ROWS, HD), 1)
    low = jnp.where(row == 2, (sums - high)[:, None], 0.0)
    rows = jnp.where(row == 0, tops[:, None], jnp.where(row == 1, high[:, None], low))
    return rows.astype(jnp.bfloat16)


def read_stats(ref):
    stats = ref[:, ref.shape[1] - 1].astype(jnp.float32)
    return stats[:, 0], stats[:, 1] + stats[:, 2]


def write_packed_stats(ref, tops, sums):
    last = ref.shape[0] - 2
    high = rounded(sums)
    ref[last] = jnp.concatenate([tops, high], axis=0).astype(jnp.bfloat16)
    ref[last + 1] = jnp.concatenate([sums - high, jnp.zeros_like(sums)], axis=0).astype(jnp.bfloat16)


def read_packed_stats(ref):
    last = ref.shape[0] - 2
    first, second = ref[last].astype(jnp.float32), ref[last + 1].astype(jnp.float32)
    return first[:8], first[8:] + second[:8]


def columns(fields):
    used = sum(f.shape[0] for f in fields)
    return jnp.concatenate(list(fields) + [jnp.zeros((HD - used, HD), jnp.float32)], axis=0).T


def prefix_kernel(factor, parts, after_ref, *refs):
    q_refs = refs[:parts]
    k_ref, v_ref = refs[parts:parts + 2]
    out_refs = refs[parts + 2:2 * parts + 2]
    top_ref, sum_ref = refs[2 * parts + 2:]
    devices, heads = q_refs[0].shape[:2]
    span = devices * ROWS
    length = k_ref.shape[0]

    def pair_part(pair, pieces, shift):
        step = length // pieces
        lanes = slice(pair * 2 * HD, (pair + 1) * 2 * HD)
        both = [q_refs[0][:, pair * 2 + j].reshape(span, HD) for j in range(2)]
        none = jnp.zeros_like(both[0])
        queries = jnp.concatenate(
            [jnp.concatenate([both[0], none], axis=1), jnp.concatenate([none, both[1]], axis=1)], axis=0
        )
        scores = [dot(k_ref[i * step:(i + 1) * step, lanes], queries, NT) for i in range(pieces)]
        top = rounded(jnp.max(scores[0][:shift], axis=0, keepdims=True))
        total = None
        for i in range(pieces):
            weights = jnp.exp2((scores[i] - top) * factor).astype(jnp.bfloat16)
            values = v_ref[i * step:(i + 1) * step, lanes]
            values = jnp.concatenate([values, jnp.ones((step, ROWS), jnp.bfloat16)], axis=1)
            more = dot(values, weights, TN)
            total = more if total is None else total + more
        for j in range(2):
            head, cols = pair * 2 + j, slice(j * span, (j + 1) * span)
            outs = total[j * HD:(j + 1) * HD, cols].T.astype(jnp.bfloat16)
            for dev in range(devices):
                out_refs[0][dev * heads + head] = outs[dev * ROWS:(dev + 1) * ROWS]
            top_ref[pl.ds(head, 1)] = top[:, cols]
            sum_ref[pl.ds(head, 1)] = total[2 * HD:2 * HD + 1, cols]

    def head_part(head, pieces, shift):
        step = length // pieces
        lanes = slice(head * HD, (head + 1) * HD) if isinstance(head, int) else pl.ds(pl.multiple_of(head * HD, HD), HD)
        queries = jnp.concatenate([r[:, head].reshape(span, HD) for r in q_refs], axis=0)
        scores = [dot(k_ref[i * step:(i + 1) * step, lanes], queries, NT) for i in range(pieces)]
        top = rounded(jnp.max(scores[0][:shift], axis=0, keepdims=True))
        total = None
        for i in range(pieces):
            weights = jnp.exp2((scores[i] - top) * factor).astype(jnp.bfloat16)
            values = v_ref[i * step:(i + 1) * step, lanes]
            values = jnp.concatenate([values, jnp.ones((step, ROWS), jnp.bfloat16)], axis=1)
            more = dot(values, weights, TN)
            total = more if total is None else total + more
        outs = total[:HD].T.astype(jnp.bfloat16)
        for i in range(parts):
            for dev in range(devices):
                first = i * span + dev * ROWS
                out_refs[i][dev * heads + head] = outs[first:first + ROWS]
        top_ref[pl.ds(head, 1)] = top
        sum_ref[pl.ds(head, 1)] = total[HD:HD + 1]

    if parts == 1:
        for pair in range(heads // 2):
            pair_part(pair, 8, 128)
    else:
        for head in range(heads):
            head_part(head, 4, 64)

    @pl.when(jnp.logical_not(jnp.max(sum_ref[...]) < 2.0 ** 64))
    def _():
        @pl.loop(0, heads)
        def _(i):
            head_part(i, 1, length)

    for i in range(parts):
        part = slice(i * span, (i + 1) * span)
        write_packed_stats(out_refs[i], by_device(top_ref[:, part]), by_device(sum_ref[:, part]))


def prefix_part(after, queries, keys, values, factor, cost=1.0):
    parts = len(queries)
    devices, heads = queries[0].shape[:2]
    length = keys.shape[0]
    rows = parts * devices * ROWS
    return pl.pallas_call(
        functools.partial(prefix_kernel, factor, parts),
        in_specs=[pl.BlockSpec(memory_space=pl.ANY)] + [VMEM] * (parts + 2),
        out_specs=[VMEM] * parts,
        out_shape=[jax.ShapeDtypeStruct((devices * heads + 2, ROWS, HD), jnp.bfloat16)] * parts,
        scratch_shapes=[pltpu.VMEM((heads, rows), jnp.float32)] * 2,
        compiler_params=pltpu.CompilerParams(vmem_limit_bytes=32 * 2**20),
        cost_estimate=pl.CostEstimate(
            flops=int(cost * 8 * rows * heads * length * HD),
            bytes_accessed=int(cost * 4 * (length + rows) * heads * HD),
            transcendentals=int(cost * rows * heads * length),
        ),
        name="prefix_part",
    )(after, *queries, keys, values)


def spread_kernel(q_ref, out_ref):
    for i in range(out_ref.shape[0]):
        out_ref[i] = q_ref[...]


def spread_part(queries, copies):
    return pl.pallas_call(
        spread_kernel,
        in_specs=[VMEM],
        out_specs=VMEM,
        out_shape=jax.ShapeDtypeStruct((copies,) + queries.shape, queries.dtype),
        compiler_params=pltpu.CompilerParams(vmem_limit_bytes=8 * 2**20),
        cost_estimate=pl.CostEstimate(flops=20 * 2**30, bytes_accessed=2**25, transcendentals=0),
        name="spread_part",
    )(queries)


def suffix_kernel(factor, len_ref, after_ref, q_ref, sk_ref, sv_ref, k_ref, v_ref, out_ref, stat_ref):
    heads = q_ref.shape[0]
    length = sk_ref.shape[1]
    odd = lax.broadcasted_iota(jnp.int32, (ROWS, length), 0) % 2 == 1
    position = lax.broadcasted_iota(jnp.int32, (ROWS, length), 1)
    valid = position < jnp.where(odd, len_ref[1], len_ref[0])
    lane = lax.broadcasted_iota(jnp.int32, (ROWS, HD), 1)
    row = lax.broadcasted_iota(jnp.int32, (ROWS, HD), 0)
    maxima = jnp.zeros((ROWS, HD), jnp.float32)
    sums = jnp.zeros((ROWS, HD), jnp.float32)
    for head in range(heads):
        cols = slice(head * HD, (head + 1) * HD)
        queries = q_ref[head]
        scores = jnp.where(odd, dot(queries, sk_ref[1, :, cols], NT), dot(queries, sk_ref[0, :, cols], NT))
        top = jnp.max(jnp.where(valid, scores, NEG_FILL), axis=1, keepdims=True)
        weights = jnp.where(valid, jnp.exp2((scores - top) * factor), 0.0).astype(jnp.bfloat16)
        total = jnp.sum(weights.astype(jnp.float32), axis=1, keepdims=True)
        outs = jnp.where(odd[:, :HD], dot(weights, sv_ref[1, :, cols], NN), dot(weights, sv_ref[0, :, cols], NN))
        out_ref[head * ROWS:(head + 1) * ROWS] = outs
        here = lane == head * ROWS + row
        maxima += jnp.where(here, top, 0.0)
        sums += jnp.where(here, total, 0.0)
    stat_ref[0:1] = jnp.sum(maxima, axis=0, keepdims=True)
    stat_ref[1:2] = jnp.sum(sums, axis=0, keepdims=True)
    stat_ref[2:] = jnp.zeros((6, HD), jnp.float32)


def suffix_part(lengths, after, queries, suffix_keys, suffix_values, keys, values, factor):
    heads = queries.shape[0]
    return pl.pallas_call(
        functools.partial(suffix_kernel, factor),
        in_specs=[pl.BlockSpec(memory_space=pltpu.SMEM), pl.BlockSpec(memory_space=pl.ANY)] + [VMEM] * 5,
        out_specs=[VMEM] * 2,
        out_shape=[
            jax.ShapeDtypeStruct((heads * ROWS, HD), jnp.float32),
            jax.ShapeDtypeStruct((8, HD), jnp.float32),
        ],
        compiler_params=pltpu.CompilerParams(vmem_limit_bytes=16 * 2**20),
        cost_estimate=pl.CostEstimate(flops=2**30, bytes_accessed=2**23, transcendentals=2**16),
        name="suffix_part",
    )(lengths, after, queries, suffix_keys, suffix_values, keys, values)


def premerge_kernel(factor, *refs):
    part_refs, (out_ref, top_ref, sum_ref) = refs[:-3], refs[-3:]
    devices = out_ref.shape[0]
    heads = out_ref.shape[1] // ROWS
    stats = [read_packed_stats(r) for r in part_refs]
    top = functools.reduce(jnp.maximum, [s[0] for s in stats])
    scales = [jnp.exp2((s[0] - top) * factor) for s in stats]
    top_ref[...] = top
    sum_ref[...] = sum(f * s[1] for f, s in zip(scales, stats))
    turned = columns(scales)
    for dev in range(devices):
        acc = None
        for i, r in enumerate(part_refs):
            block = r[dev * heads:(dev + 1) * heads].reshape(heads * ROWS, HD).astype(jnp.float32)
            term = block * turned[:, i * devices + dev:i * devices + dev + 1]
            acc = term if acc is None else acc + term
        out_ref[dev] = acc


def premerge_part(parts, factor):
    heads = parts[0].shape[0] // Z
    return pl.pallas_call(
        functools.partial(premerge_kernel, factor),
        in_specs=[VMEM] * len(parts),
        out_specs=[VMEM] * 3,
        out_shape=[
            jax.ShapeDtypeStruct((Z, heads * ROWS, HD), jnp.float32),
            jax.ShapeDtypeStruct((Z, HD), jnp.float32),
            jax.ShapeDtypeStruct((Z, HD), jnp.float32),
        ],
        compiler_params=pltpu.CompilerParams(vmem_limit_bytes=16 * 2**20),
        name="premerge_part",
    )(*parts)


def merge_kernel(factor, acc_ref, acc_top_ref, acc_sum_ref, last_ref, out_ref):
    devices = out_ref.shape[0]
    heads = out_ref.shape[1] - 1
    last_top, last_sum = read_packed_stats(last_ref)
    top = jnp.maximum(acc_top_ref[...], last_top)
    scales = [jnp.exp2((t - top) * factor) for t in (acc_top_ref[...], last_top)]
    rows = stat_rows(top, scales[0] * acc_sum_ref[...] + scales[1] * last_sum)
    turned = columns(scales)
    for dev in range(devices):
        block = last_ref[dev * heads:(dev + 1) * heads].reshape(heads * ROWS, HD).astype(jnp.float32)
        acc = acc_ref[dev] * turned[:, dev:dev + 1] + block * turned[:, devices + dev:devices + dev + 1]
        out_ref[dev, :heads] = acc.astype(jnp.bfloat16).reshape(heads, ROWS, HD)
        out_ref[dev, heads] = rows[dev]


def merge_part(merged, last, factor):
    return pl.pallas_call(
        functools.partial(merge_kernel, factor),
        in_specs=[VMEM] * (len(merged) + 1),
        out_specs=VMEM,
        out_shape=jax.ShapeDtypeStruct((Z, last.shape[0] // Z + 1, ROWS, HD), jnp.bfloat16),
        compiler_params=pltpu.CompilerParams(vmem_limit_bytes=16 * 2**20),
        name="merge_part",
    )(*merged, last)


def combine_kernel(factor, got_ref, suf_ref, stat_ref, out_ref):
    devices = got_ref.shape[0]
    heads = got_ref.shape[1] - 1
    tops, sums = read_stats(got_ref)
    suf_top = stat_ref[0:1]
    top = jnp.maximum(jnp.max(tops, axis=0, keepdims=True), suf_top)
    scale = jnp.exp2((tops - top) * factor)
    suf_scale = jnp.exp2((suf_top - top) * factor)
    total = jnp.sum(scale * sums, axis=0, keepdims=True) + suf_scale * stat_ref[1:2]
    shares = columns([scale / total, suf_scale / total])
    acc = suf_ref[...] * shares[:, devices:devices + 1]
    for src in range(devices):
        block = got_ref[src, :heads].reshape(heads * ROWS, HD).astype(jnp.float32)
        acc += block * shares[:, src:src + 1]
    out_ref[...] = acc.astype(jnp.bfloat16)


def combine_part(got, suf_out, suf_stats, factor):
    return pl.pallas_call(
        functools.partial(combine_kernel, factor),
        in_specs=[VMEM, VMEM, VMEM],
        out_specs=VMEM,
        out_shape=jax.ShapeDtypeStruct(suf_out.shape, jnp.bfloat16),
        compiler_params=pltpu.CompilerParams(vmem_limit_bytes=16 * 2**20),
        name="combine_part",
    )(got, suf_out, suf_stats)


def shift_x(array, by):
    pairs = [(z * X + x, z * X + (x + by) % X) for z in range(Z) for x in range(X)]
    return lax.ppermute(array, "ctx", pairs)


def swap_z(array):
    groups = [[z * X + x for z in range(Z)] for x in range(X)]
    return lax.all_to_all(array, "ctx", 0, 0, axis_index_groups=groups, tiled=True)


def local(queries, prefix_keys, prefix_values, suffix_keys, suffix_values, suffix_len):
    owned, width = queries.shape
    heads = prefix_keys.shape[1] // HD
    factor = LOG2E * HD ** -0.5
    mine = queries.reshape(owned, heads, 8, HD).transpose(1, 2, 0, 3).reshape(heads, ROWS, HD)
    column = swap_z(spread_part(mine, Z))
    before, after = shift_x(column, 1), shift_x(column, -1)
    suf_out, suf_stats = suffix_part(
        suffix_len, column, mine, suffix_keys, suffix_values, prefix_keys, prefix_values, factor
    )
    across = shift_x(before, 1)
    for_before, for_after = prefix_part(suf_stats, [before, after], prefix_keys, prefix_values, factor)
    from_after, from_before = shift_x(for_before, -1), shift_x(for_after, 1)
    [for_across] = prefix_part(for_before, [across], prefix_keys, prefix_values, factor)
    from_across = shift_x(for_across, 2)
    [for_own] = prefix_part(for_across, [column], prefix_keys, prefix_values, factor, cost=0.01)
    early = premerge_part([for_own, from_after, from_before], factor)
    merged = merge_part(early, from_across, factor)
    got = swap_z(merged)
    out = combine_part(got, suf_out, suf_stats, factor)
    return out.reshape(heads * 8, owned, HD).transpose(1, 0, 2).reshape(owned, width)


def solution(mesh):
    placed = (
        P(("grp", "ctx"), None),
        P(("grp", "ctx"), None),
        P(("grp", "ctx"), None),
        P(("grp", "ctx"), None, None),
        P(("grp", "ctx"), None, None),
        P(("grp", "ctx")),
    )
    return jax.shard_map(
        local, mesh=mesh, in_specs=placed, out_specs=P(("grp", "ctx"), None), check_vma=False
    )
```

```python
import functools

import jax
import jax.numpy as jnp
from jax import lax
from jax.experimental import pallas as pl
from jax.experimental.pallas import tpu as pltpu
from jax.sharding import PartitionSpec as P

HD = 128
LOG2E = 1.4426950408889634
NEG_FILL = -1e30
ROWS = 16
Z, X = 8, 4

NT = (((1,), (1,)), ((), ()))
NN = (((1,), (0,)), ((), ()))
TN = (((0,), (0,)), ((), ()))
VMEM = pl.BlockSpec(memory_space=pltpu.VMEM)


def dot(a, b, dims):
    return lax.dot_general(a, b, dims, preferred_element_type=jnp.float32)


def rounded(x):
    return x.astype(jnp.bfloat16).astype(jnp.float32)


def by_device(field):
    row = lax.broadcasted_iota(jnp.int32, (8, HD), 0)
    group = lax.broadcasted_iota(jnp.int32, (8, HD), 1) // ROWS
    turn = (row - group) % 8
    out = field
    for k in range(1, 8):
        moved = pltpu.roll(pltpu.roll(field, k, 0), HD - ROWS * k, 1)
        out = jnp.where(turn == k, moved, out)
    return out


def stat_rows(tops, sums):
    devices = tops.shape[0]
    high = rounded(sums)
    row = lax.broadcasted_iota(jnp.int32, (devices, ROWS, HD), 1)
    low = jnp.where(row == 2, (sums - high)[:, None], 0.0)
    rows = jnp.where(row == 0, tops[:, None], jnp.where(row == 1, high[:, None], low))
    return rows.astype(jnp.bfloat16)


def read_stats(ref):
    stats = ref[:, ref.shape[1] - 1].astype(jnp.float32)
    return stats[:, 0], stats[:, 1] + stats[:, 2]


def write_packed_stats(ref, tops, sums):
    last = ref.shape[0] - 2
    high = rounded(sums)
    ref[last] = jnp.concatenate([tops, high], axis=0).astype(jnp.bfloat16)
    ref[last + 1] = jnp.concatenate([sums - high, jnp.zeros_like(sums)], axis=0).astype(jnp.bfloat16)


def read_packed_stats(ref):
    last = ref.shape[0] - 2
    first, second = ref[last].astype(jnp.float32), ref[last + 1].astype(jnp.float32)
    return first[:8], first[8:] + second[:8]


def columns(fields):
    used = sum(f.shape[0] for f in fields)
    return jnp.concatenate(list(fields) + [jnp.zeros((HD - used, HD), jnp.float32)], axis=0).T


def prefix_kernel(factor, parts, after_ref, *refs):
    q_refs = refs[:parts]
    k_ref, v_ref = refs[parts:parts + 2]
    out_refs = refs[parts + 2:2 * parts + 2]
    top_ref, sum_ref = refs[2 * parts + 2:]
    devices, heads = q_refs[0].shape[:2]
    span = devices * ROWS
    length = k_ref.shape[0]

    def pair_part(pair, pieces, shift):
        step = length // pieces
        lanes = slice(pair * 2 * HD, (pair + 1) * 2 * HD)
        both = [q_refs[0][:, pair * 2 + j].reshape(span, HD) for j in range(2)]
        none = jnp.zeros_like(both[0])
        queries = jnp.concatenate(
            [jnp.concatenate([both[0], none], axis=1), jnp.concatenate([none, both[1]], axis=1)], axis=0
        )
        scores = [dot(k_ref[i * step:(i + 1) * step, lanes], queries, NT) for i in range(pieces)]
        top = rounded(jnp.max(scores[0][:shift], axis=0, keepdims=True))
        total = None
        for i in range(pieces):
            weights = jnp.exp2((scores[i] - top) * factor).astype(jnp.bfloat16)
            values = v_ref[i * step:(i + 1) * step, lanes]
            values = jnp.concatenate([values, jnp.ones((step, ROWS), jnp.bfloat16)], axis=1)
            more = dot(values, weights, TN)
            total = more if total is None else total + more
        for j in range(2):
            head, cols = pair * 2 + j, slice(j * span, (j + 1) * span)
            outs = total[j * HD:(j + 1) * HD, cols].T.astype(jnp.bfloat16)
            for dev in range(devices):
                out_refs[0][dev * heads + head] = outs[dev * ROWS:(dev + 1) * ROWS]
            top_ref[pl.ds(head, 1)] = top[:, cols]
            sum_ref[pl.ds(head, 1)] = total[2 * HD:2 * HD + 1, cols]

    def head_part(head, pieces, shift):
        step = length // pieces
        lanes = slice(head * HD, (head + 1) * HD) if isinstance(head, int) else pl.ds(pl.multiple_of(head * HD, HD), HD)
        queries = jnp.concatenate([r[:, head].reshape(span, HD) for r in q_refs], axis=0)
        scores = [dot(k_ref[i * step:(i + 1) * step, lanes], queries, NT) for i in range(pieces)]
        top = rounded(jnp.max(scores[0][:shift], axis=0, keepdims=True))
        total = None
        for i in range(pieces):
            weights = jnp.exp2((scores[i] - top) * factor).astype(jnp.bfloat16)
            values = v_ref[i * step:(i + 1) * step, lanes]
            values = jnp.concatenate([values, jnp.ones((step, ROWS), jnp.bfloat16)], axis=1)
            more = dot(values, weights, TN)
            total = more if total is None else total + more
        outs = total[:HD].T.astype(jnp.bfloat16)
        for i in range(parts):
            for dev in range(devices):
                first = i * span + dev * ROWS
                out_refs[i][dev * heads + head] = outs[first:first + ROWS]
        top_ref[pl.ds(head, 1)] = top
        sum_ref[pl.ds(head, 1)] = total[HD:HD + 1]

    if parts == 1:
        for pair in range(heads // 2):
            pair_part(pair, 8, 128)
    else:
        for head in range(heads):
            head_part(head, 4, 16)

    @pl.when(jnp.logical_not(jnp.max(sum_ref[...]) < 2.0 ** 64))
    def _():
        @pl.loop(0, heads)
        def _(i):
            head_part(i, 1, length)

    for i in range(parts):
        part = slice(i * span, (i + 1) * span)
        write_packed_stats(out_refs[i], by_device(top_ref[:, part]), by_device(sum_ref[:, part]))


def prefix_part(after, queries, keys, values, factor, cost=1.0):
    parts = len(queries)
    devices, heads = queries[0].shape[:2]
    length = keys.shape[0]
    rows = parts * devices * ROWS
    return pl.pallas_call(
        functools.partial(prefix_kernel, factor, parts),
        in_specs=[pl.BlockSpec(memory_space=pl.ANY)] + [VMEM] * (parts + 2),
        out_specs=[VMEM] * parts,
        out_shape=[jax.ShapeDtypeStruct((devices * heads + 2, ROWS, HD), jnp.bfloat16)] * parts,
        scratch_shapes=[pltpu.VMEM((heads, rows), jnp.float32)] * 2,
        compiler_params=pltpu.CompilerParams(vmem_limit_bytes=32 * 2**20),
        cost_estimate=pl.CostEstimate(
            flops=int(cost * 8 * rows * heads * length * HD),
            bytes_accessed=int(cost * 4 * (length + rows) * heads * HD),
            transcendentals=int(cost * rows * heads * length),
        ),
        name="prefix_part",
    )(after, *queries, keys, values)


def spread_kernel(q_ref, out_ref):
    for i in range(out_ref.shape[0]):
        out_ref[i] = q_ref[...]


def spread_part(queries, copies):
    return pl.pallas_call(
        spread_kernel,
        in_specs=[VMEM],
        out_specs=VMEM,
        out_shape=jax.ShapeDtypeStruct((copies,) + queries.shape, queries.dtype),
        compiler_params=pltpu.CompilerParams(vmem_limit_bytes=8 * 2**20),
        cost_estimate=pl.CostEstimate(flops=20 * 2**30, bytes_accessed=2**25, transcendentals=0),
        name="spread_part",
    )(queries)


def suffix_kernel(factor, len_ref, after_ref, q_ref, sk_ref, sv_ref, k_ref, v_ref, out_ref, stat_ref):
    heads = q_ref.shape[0]
    length = sk_ref.shape[1]
    odd = lax.broadcasted_iota(jnp.int32, (ROWS, length), 0) % 2 == 1
    position = lax.broadcasted_iota(jnp.int32, (ROWS, length), 1)
    valid = position < jnp.where(odd, len_ref[1], len_ref[0])
    lane = lax.broadcasted_iota(jnp.int32, (ROWS, HD), 1)
    row = lax.broadcasted_iota(jnp.int32, (ROWS, HD), 0)
    maxima = jnp.zeros((ROWS, HD), jnp.float32)
    sums = jnp.zeros((ROWS, HD), jnp.float32)
    for head in range(heads):
        cols = slice(head * HD, (head + 1) * HD)
        queries = q_ref[head]
        scores = jnp.where(odd, dot(queries, sk_ref[1, :, cols], NT), dot(queries, sk_ref[0, :, cols], NT))
        top = jnp.max(jnp.where(valid, scores, NEG_FILL), axis=1, keepdims=True)
        weights = jnp.where(valid, jnp.exp2((scores - top) * factor), 0.0).astype(jnp.bfloat16)
        total = jnp.sum(weights.astype(jnp.float32), axis=1, keepdims=True)
        outs = jnp.where(odd[:, :HD], dot(weights, sv_ref[1, :, cols], NN), dot(weights, sv_ref[0, :, cols], NN))
        out_ref[head * ROWS:(head + 1) * ROWS] = outs
        here = lane == head * ROWS + row
        maxima += jnp.where(here, top, 0.0)
        sums += jnp.where(here, total, 0.0)
    stat_ref[0:1] = jnp.sum(maxima, axis=0, keepdims=True)
    stat_ref[1:2] = jnp.sum(sums, axis=0, keepdims=True)
    stat_ref[2:] = jnp.zeros((6, HD), jnp.float32)


def suffix_part(lengths, after, queries, suffix_keys, suffix_values, keys, values, factor):
    heads = queries.shape[0]
    return pl.pallas_call(
        functools.partial(suffix_kernel, factor),
        in_specs=[pl.BlockSpec(memory_space=pltpu.SMEM), pl.BlockSpec(memory_space=pl.ANY)] + [VMEM] * 5,
        out_specs=[VMEM] * 2,
        out_shape=[
            jax.ShapeDtypeStruct((heads * ROWS, HD), jnp.float32),
            jax.ShapeDtypeStruct((8, HD), jnp.float32),
        ],
        compiler_params=pltpu.CompilerParams(vmem_limit_bytes=16 * 2**20),
        cost_estimate=pl.CostEstimate(flops=2**30, bytes_accessed=2**23, transcendentals=2**16),
        name="suffix_part",
    )(lengths, after, queries, suffix_keys, suffix_values, keys, values)


def premerge_kernel(factor, *refs):
    part_refs, (out_ref, top_ref, sum_ref) = refs[:-3], refs[-3:]
    devices = out_ref.shape[0]
    heads = out_ref.shape[1] // ROWS
    stats = [read_packed_stats(r) for r in part_refs]
    top = functools.reduce(jnp.maximum, [s[0] for s in stats])
    scales = [jnp.exp2((s[0] - top) * factor) for s in stats]
    top_ref[...] = top
    sum_ref[...] = sum(f * s[1] for f, s in zip(scales, stats))
    turned = columns(scales)
    for dev in range(devices):
        acc = None
        for i, r in enumerate(part_refs):
            block = r[dev * heads:(dev + 1) * heads].reshape(heads * ROWS, HD).astype(jnp.float32)
            term = block * turned[:, i * devices + dev:i * devices + dev + 1]
            acc = term if acc is None else acc + term
        out_ref[dev] = acc


def premerge_part(parts, factor):
    heads = parts[0].shape[0] // Z
    return pl.pallas_call(
        functools.partial(premerge_kernel, factor),
        in_specs=[VMEM] * len(parts),
        out_specs=[VMEM] * 3,
        out_shape=[
            jax.ShapeDtypeStruct((Z, heads * ROWS, HD), jnp.float32),
            jax.ShapeDtypeStruct((Z, HD), jnp.float32),
            jax.ShapeDtypeStruct((Z, HD), jnp.float32),
        ],
        compiler_params=pltpu.CompilerParams(vmem_limit_bytes=16 * 2**20),
        name="premerge_part",
    )(*parts)


def merge_kernel(factor, acc_ref, acc_top_ref, acc_sum_ref, last_ref, out_ref):
    devices = out_ref.shape[0]
    heads = out_ref.shape[1] - 1
    last_top, last_sum = read_packed_stats(last_ref)
    top = jnp.maximum(acc_top_ref[...], last_top)
    scales = [jnp.exp2((t - top) * factor) for t in (acc_top_ref[...], last_top)]
    rows = stat_rows(top, scales[0] * acc_sum_ref[...] + scales[1] * last_sum)
    turned = columns(scales)
    for dev in range(devices):
        block = last_ref[dev * heads:(dev + 1) * heads].reshape(heads * ROWS, HD).astype(jnp.float32)
        acc = acc_ref[dev] * turned[:, dev:dev + 1] + block * turned[:, devices + dev:devices + dev + 1]
        out_ref[dev, :heads] = acc.astype(jnp.bfloat16).reshape(heads, ROWS, HD)
        out_ref[dev, heads] = rows[dev]


def merge_part(merged, last, factor):
    return pl.pallas_call(
        functools.partial(merge_kernel, factor),
        in_specs=[VMEM] * (len(merged) + 1),
        out_specs=VMEM,
        out_shape=jax.ShapeDtypeStruct((Z, last.shape[0] // Z + 1, ROWS, HD), jnp.bfloat16),
        compiler_params=pltpu.CompilerParams(vmem_limit_bytes=16 * 2**20),
        name="merge_part",
    )(*merged, last)


def combine_kernel(factor, got_ref, suf_ref, stat_ref, out_ref):
    devices = got_ref.shape[0]
    heads = got_ref.shape[1] - 1
    tops, sums = read_stats(got_ref)
    suf_top = stat_ref[0:1]
    top = jnp.maximum(jnp.max(tops, axis=0, keepdims=True), suf_top)
    scale = jnp.exp2((tops - top) * factor)
    suf_scale = jnp.exp2((suf_top - top) * factor)
    total = jnp.sum(scale * sums, axis=0, keepdims=True) + suf_scale * stat_ref[1:2]
    shares = columns([scale / total, suf_scale / total])
    acc = suf_ref[...] * shares[:, devices:devices + 1]
    for src in range(devices):
        block = got_ref[src, :heads].reshape(heads * ROWS, HD).astype(jnp.float32)
        acc += block * shares[:, src:src + 1]
    out_ref[...] = acc.astype(jnp.bfloat16)


def combine_part(got, suf_out, suf_stats, factor):
    return pl.pallas_call(
        functools.partial(combine_kernel, factor),
        in_specs=[VMEM, VMEM, VMEM],
        out_specs=VMEM,
        out_shape=jax.ShapeDtypeStruct(suf_out.shape, jnp.bfloat16),
        compiler_params=pltpu.CompilerParams(vmem_limit_bytes=16 * 2**20),
        name="combine_part",
    )(got, suf_out, suf_stats)


def shift_x(array, by):
    pairs = [(z * X + x, z * X + (x + by) % X) for z in range(Z) for x in range(X)]
    return lax.ppermute(array, "ctx", pairs)


def swap_z(array):
    groups = [[z * X + x for z in range(Z)] for x in range(X)]
    return lax.all_to_all(array, "ctx", 0, 0, axis_index_groups=groups, tiled=True)


def local(queries, prefix_keys, prefix_values, suffix_keys, suffix_values, suffix_len):
    owned, width = queries.shape
    heads = prefix_keys.shape[1] // HD
    factor = LOG2E * HD ** -0.5
    mine = queries.reshape(owned, heads, 8, HD).transpose(1, 2, 0, 3).reshape(heads, ROWS, HD)
    column = swap_z(spread_part(mine, Z))
    before, after = shift_x(column, 1), shift_x(column, -1)
    suf_out, suf_stats = suffix_part(
        suffix_len, column, mine, suffix_keys, suffix_values, prefix_keys, prefix_values, factor
    )
    across = shift_x(before, 1)
    for_before, for_after = prefix_part(suf_stats, [before, after], prefix_keys, prefix_values, factor)
    from_after, from_before = shift_x(for_before, -1), shift_x(for_after, 1)
    [for_across] = prefix_part(for_before, [across], prefix_keys, prefix_values, factor)
    from_across = shift_x(for_across, 2)
    [for_own] = prefix_part(for_across, [column], prefix_keys, prefix_values, factor, cost=0.01)
    early = premerge_part([for_own, from_after, from_before], factor)
    merged = merge_part(early, from_across, factor)
    got = swap_z(merged)
    out = combine_part(got, suf_out, suf_stats, factor)
    return out.reshape(heads * 8, owned, HD).transpose(1, 0, 2).reshape(owned, width)


def solution(mesh):
    placed = (
        P(("grp", "ctx"), None),
        P(("grp", "ctx"), None),
        P(("grp", "ctx"), None),
        P(("grp", "ctx"), None, None),
        P(("grp", "ctx"), None, None),
        P(("grp", "ctx")),
    )
    return jax.shard_map(
        local, mesh=mesh, in_specs=placed, out_specs=P(("grp", "ctx"), None), check_vma=False
    )
```
